32 devices in a mesh: gx: 16 (over z, x, core), gy: 2 (over y).
Axes of the slice: x: 2, y: 2, z: 4, core: 2. Of those that a mesh axis runs over, the one named last changes fastest.
Arguments:
- labels: int32 [1, 2048, 2048], P(None, 'gx', 'gy'), may hold values from 0 to 2
- damage: float32 [1, 2048, 2048], P(None, 'gx', 'gy'), may hold values from -6 to 6
- opening: float32 [1, 2048, 2048], P(None, 'gx', 'gy'), may hold values from -6 to 6
- strain: float32 [3, 1, 2048, 2048], P(None, None, 'gx', 'gy'), may hold values from -6 to 6
Outputs:
- correlations: float32 [21, 1, 2048, 2048], P(None, None, 'gx', 'gy')
The draws below stay inside these ranges and needn't reach their ends.
All inputs are finite; a program needn't handle non-finite values.
Results may differ from the reference program's by a relative error of at most 0.00013.
Values sent between devices are 32-bit elements; how exact they have to be, the bound alone decides.
A program may use at most 192 MiB of HBM per device.

```python
import jax
import jax.numpy as jnp

GRID = 2048
FIELDS = 6
PLANES = 1


def set_ends(drawn, stream_key, least, largest):
    place = [jax.random.randint(jax.random.fold_in(stream_key, axis), (), 0, length) for axis, length in enumerate(drawn.shape)]
    longest = drawn.shape.index(max(drawn.shape))
    beside = place[:longest] + [(place[longest] + 1) % drawn.shape[longest]] + place[longest + 1:]
    return drawn.at[tuple(place)].set(least).at[tuple(beside)].set(largest)


def shard_levels(rng, shape, split, least, top_value):
    factor_of = 1.0
    for axis_at, blocks in split:
        heights = jax.random.uniform(jax.random.fold_in(jax.random.fold_in(rng, 6), axis_at), (blocks,), jnp.float32, least / len(split), top_value / len(split))
        factor_of = factor_of * jnp.repeat(jnp.exp(heights), shape[axis_at] // blocks).reshape((-1,) + (1,) * (len(shape) - 1 - axis_at))
    return factor_of


def noise(key, extent, spread, bound, split=(), kind=jnp.bfloat16):
    gain = shard_levels(key, extent, split, -0.22, 0.18) if split else 1.0
    drawn = jax.random.normal(key, extent, jnp.float32) * spread * gain
    return jnp.minimum(jnp.maximum(drawn, -bound), bound).astype(kind)


def setup_inputs(seed: int = 0) -> dict:
    keys = jax.random.split(jax.random.key(seed), 5)
    return {
        "labels": set_ends(jax.random.randint(keys[0], (PLANES, GRID, GRID), 0, 3), jax.random.fold_in(keys[0], 1), 0, 2).astype(jnp.int32),
        "damage": noise(keys[1], (PLANES, GRID, GRID), 1.0, 6.0, ((1, 16), (2, 2)), jnp.float32),
        "opening": noise(keys[2], (PLANES, GRID, GRID), 1.0, 6.0, ((1, 16), (2, 2)), jnp.float32),
        "strain": noise(keys[3], (3, PLANES, GRID, GRID), 1.0, 6.0, ((2, 16), (3, 2)), jnp.float32),
    }


def reference(labels, damage, opening, strain):
    phase_field = labels.astype(jnp.float32) - 1.0
    fields = jnp.concatenate([phase_field[None], damage[None], opening[None], strain], axis=0)
    spectra = jnp.fft.fft2(fields, axes=(-2, -1))
    outputs = []
    for left_field in range(FIELDS):
        for right_field in range(left_field, FIELDS):
            cross_spectrum = jnp.conj(spectra[left_field]) * spectra[right_field]
            inverse = jnp.fft.ifft2(cross_spectrum, axes=(-2, -1)).real / GRID
            outputs.append(inverse.astype(jnp.float32))
    return jnp.stack(outputs)
```

```python
import functools
import math

import jax
import jax.numpy as jnp
import ml_dtypes
import numpy as np
from jax import lax
from jax.experimental import pallas as pl
from jax.experimental.pallas import tpu as pltpu
from jax.sharding import PartitionSpec as P

GRID = 2048


HIGHEST = lax.Precision.HIGHEST


def phase_table(row_count, col_count, length, orient):
    row_index = lax.broadcasted_iota(jnp.int32, (row_count, col_count), 0)
    col_index = lax.broadcasted_iota(jnp.int32, (row_count, col_count), 1)
    angles = (row_index * col_index % length).astype(jnp.float32) * (2.0 * math.pi / length)
    return (jnp.cos(angles), orient * jnp.sin(angles))


def contract(stacked, factors, pattern):
    cosine, sine_part = factors

    def product(values, matrix):
        return jnp.einsum(
            pattern, values, matrix, precision=HIGHEST, preferred_element_type=jnp.float32
        )

    if stacked.shape[0] == 1:
        return jnp.stack([product(stacked[0], cosine), product(stacked[0], sine_part)])
    real_part, imag_part = (stacked[0], stacked[1])
    return jnp.stack(
        [
            product(real_part, cosine) - product(imag_part, sine_part),
            product(real_part, sine_part) + product(imag_part, cosine),
        ]
    )


def rotate(stacked, factors):
    cosine, sine_part = factors
    real_part, imag_part = (stacked[0], stacked[1])
    return jnp.stack(
        [real_part * cosine - imag_part * sine_part, real_part * sine_part + imag_part * cosine]
    )


def y_transform(stacked, orient):
    members, item_count, line_count, length = stacked.shape
    minor_size = 128
    major_size = length // minor_size
    blocks = stacked.reshape(members, item_count, line_count, major_size, minor_size)
    if orient < 0:
        blocks = contract(
            blocks, phase_table(major_size, major_size, major_size, orient), "bmuv,ku->bmkv"
        )
        blocks = rotate(blocks, phase_table(major_size, minor_size, length, orient))
        blocks = contract(
            blocks, phase_table(minor_size, minor_size, minor_size, orient), "bmkv,vn->bmkn"
        )
    else:
        blocks = contract(
            blocks, phase_table(minor_size, minor_size, minor_size, orient), "bmkn,nv->bmkv"
        )
        blocks = rotate(blocks, phase_table(major_size, minor_size, length, orient))
        blocks = contract(
            blocks, phase_table(major_size, major_size, major_size, orient), "bmkv,ku->bmuv"
        )
    return blocks.reshape(2, item_count, line_count, length)


def x_transform(stacked, orient):
    members, item_count, row_count, col_count = stacked.shape
    devices = lax.axis_size("gx")
    piece_size = row_count * col_count // devices
    device_index = lax.axis_index("gx")
    grid_size = row_count * devices
    frequency = lax.broadcasted_iota(jnp.int32, (devices, piece_size), 0)
    offset = lax.broadcasted_iota(jnp.int32, (devices, piece_size), 1)
    position = (device_index * piece_size + offset) // col_count
    angles = (position * frequency % grid_size).astype(jnp.float32) * (2.0 * math.pi / grid_size)
    twiddle = (jnp.cos(angles), orient * jnp.sin(angles))
    square = phase_table(devices, devices, devices, orient)
    if orient > 0:
        stacked = contract(
            stacked, phase_table(row_count, row_count, row_count, orient), "bkp,kr->brp"
        )

    def spread_work(received):
        if orient < 0:
            return rotate(contract(received, square, "bal,ka->bkl"), twiddle)
        return contract(rotate(received, twiddle), square, "bkl,ka->bal")

    spread = spread_work(
        lax.all_to_all(
            stacked.reshape(stacked.shape[0], item_count, devices, piece_size),
            "gx",
            split_axis=2,
            concat_axis=2,
            tiled=True,
        )
    )

    def collect_work(received):
        shaped = received.reshape(received.shape[0], received.shape[1], row_count, col_count)
        if orient < 0:
            return contract(
                shaped, phase_table(row_count, row_count, row_count, orient), "brp,kr->bkp"
            )
        return shaped

    return collect_work(lax.all_to_all(spread, "gx", split_axis=2, concat_axis=3, tiled=True))


def pencil_open(stacked, orient):
    return y_transform(
        lax.all_to_all(stacked, "gy", split_axis=2, concat_axis=3, tiled=True), orient
    )


def pencil_close(stacked):
    return lax.all_to_all(stacked, "gy", split_axis=3, concat_axis=2, tiled=True)


def pair_spectra(spectra, field_count, planes):
    members, item_count, line_count, length = spectra.shape
    shaped = spectra.reshape(2, field_count, planes, line_count, length)
    real_part, imag_part = (shaped[0], shaped[1])
    crosses = []
    for left_field in range(field_count):
        for right_field in range(left_field, field_count):
            crosses.append(
                (
                    real_part[left_field] * real_part[right_field]
                    + imag_part[left_field] * imag_part[right_field],
                    real_part[left_field] * imag_part[right_field]
                    - imag_part[left_field] * real_part[right_field],
                )
            )
    nothing = jnp.zeros_like(real_part[0])
    crosses.append((nothing, nothing))
    packed_real = []
    packed_imag = []
    for number in range(0, len(crosses), 2):
        even_pair = crosses[number]
        odd_pair = crosses[number + 1]
        packed_real.append(even_pair[0] - odd_pair[1])
        packed_imag.append(even_pair[1] + odd_pair[0])
    return jnp.stack([jnp.stack(packed_real), jnp.stack(packed_imag)]).reshape(
        2, -1, line_count, length
    )


def plain_local(labels, damage, opening, strain):
    phase_field = labels.astype(jnp.float32) - 1.0
    fields = jnp.concatenate([phase_field[None], damage[None], opening[None], strain], axis=0)
    field_count, planes, row_count, col_count = fields.shape
    stacked = fields.reshape(1, field_count * planes, row_count, col_count)
    spectra = pencil_open(x_transform(stacked, -1.0), -1.0)
    packed = pair_spectra(spectra, field_count, planes)
    result = x_transform(pencil_close(y_transform(packed, 1.0)), 1.0)
    pair_count = field_count * (field_count + 1) // 2
    shaped = result.reshape(2, -1, planes, row_count, col_count)
    alternated = jnp.stack([shaped[0], shaped[1]], axis=1).reshape(-1, planes, row_count, col_count)
    scale = 1.0 / (float(GRID) * float(GRID) * float(GRID))
    return alternated[:pair_count] * scale


RADIX = 8
PART = GRID // RADIX
FIELD_COUNT = 6
KEEP = 32
ROOT = math.sqrt(0.5)
PAIRS = [(i, j) for i in range(FIELD_COUNT) for j in range(i, FIELD_COUNT)]
CHUNKS = ((0, 4), (4, 8), (8, 11))
VMEM_BYTES = 56 * 1024 * 1024


def split_table(table):
    high = table.astype(np.float32).astype(ml_dtypes.bfloat16)
    low = (table - high.astype(np.float64)).astype(np.float32).astype(ml_dtypes.bfloat16)
    return np.stack([high, low])


def angle_table(first):
    b = np.arange(PART)[:, None]
    k2 = np.arange(PART)[None, :]
    return 2.0 * np.pi * ((b * (first + RADIX * k2)) % GRID) / GRID


def lane_order(values_real, values_imag):
    rows, count = values_real.shape
    both = np.stack([values_real.reshape(rows, -1, KEEP), values_imag.reshape(rows, -1, KEEP)], axis=2)
    return both.reshape(rows, 2 * count)


@functools.lru_cache(maxsize=None)
def tables():
    half = PART // 2
    small, large, small_back, large_back = [], [], [], []
    for first in (0, 4):
        angle = angle_table(first)[:, :half]
        cosine, sine = np.cos(angle), np.sin(angle)
        forward_imag = -sine
        back_real, back_imag = 2.0 * cosine, -2.0 * sine
        if first == 0:
            alternating = np.cos(np.pi * np.arange(PART))
            forward_imag[:, 0] = alternating
            back_real[:, 0] = 1.0
            back_imag[:, 0] = alternating
        small.append(lane_order(cosine, forward_imag))
        small_back.append(lane_order(back_real, back_imag).T)
    for first in (1, 2, 3):
        angle = angle_table(first)
        cosine, sine = np.cos(angle), np.sin(angle)
        large.append(np.concatenate([lane_order(cosine, -sine), lane_order(sine, cosine)], axis=0))
        large_back.append(
            2.0
            * np.concatenate([lane_order(cosine, -sine).T, lane_order(sine, cosine).T], axis=1)
        )
    scale = 1.0 / (float(GRID) * float(GRID) * float(GRID))
    across, across_back = [], []
    for first in range(RADIX):
        angle = angle_table(first)
        cosine, sine = np.cos(angle), np.sin(angle)
        across.append(np.concatenate([cosine.T, sine.T], axis=1))
        across_back.append(np.concatenate([cosine, -sine], axis=1))
    return tuple(
        split_table(np.stack(group))
        for group in (
            small,
            large,
            [scale * table for table in small_back],
            [scale * table for table in large_back],
            across,
            across_back,
        )
    )


def halves(values):
    high = values.astype(jnp.bfloat16)
    low = (values - high.astype(jnp.float32)).astype(jnp.bfloat16)
    return high, low


def dot(left, right):
    return jnp.dot(left, right, preferred_element_type=jnp.float32)


def times_table(values, table_high, table_low):
    high, low = halves(values)
    return dot(high, table_high) + (dot(low, table_high) + dot(high, table_low))


def table_times(table_high, table_low, values):
    high, low = halves(values)
    return dot(table_high, high) + (dot(table_high, low) + dot(table_low, high))


def lane_mask(shape, period, first):
    return lax.broadcasted_iota(jnp.int32, shape, 1) % period < first


def minus_i(values):
    real_lane = lane_mask(values.shape, 2 * KEEP, KEEP)
    width = values.shape[1]
    return jnp.where(
        real_lane, pltpu.roll(values, width - KEEP, 1), -pltpu.roll(values, KEEP, 1)
    )


def eight(parts, turn):
    e = [parts[a] + parts[a + 4] for a in range(4)]
    d = [parts[a] - parts[a + 4] for a in range(4)]
    even, odd = e[0] + e[2], e[1] + e[3]
    twist = turn(e[1] - e[3])
    flat = e[0] - e[2]
    cross = turn(d[2])
    near, far = d[0] + cross, d[0] - cross
    span = turn(d[1] + d[3])
    gap = d[1] - d[3]
    first, third = ROOT * (span + gap), ROOT * (span - gap)
    return [
        even + odd,
        near + first,
        flat + twist,
        far + third,
        even - odd,
        near - first,
        flat - twist,
        far - third,
    ]


def rows_kernel(x_ref, small_ref, large_ref, out_ref, wide):
    parts_count, fields, rows, cols = x_ref.shape
    per = cols // PART
    count = fields * rows

    def part(a):
        return x_ref[a // per, :, :, (a % per) * PART : (a % per + 1) * PART].reshape(count, PART)

    s = [part(a) for a in range(RADIX)]
    e = [s[a] + s[a + 4] for a in range(4)]
    d = [s[a] - s[a + 4] for a in range(4)]
    even, odd = e[0] + e[2], e[1] + e[3]
    gap, both = ROOT * (d[1] - d[3]), ROOT * (d[1] + d[3])
    wide[:, 0:PART] = times_table(even + odd, small_ref[0, 0], small_ref[1, 0])
    wide[:, PART : 2 * PART] = times_table(even - odd, small_ref[0, 1], small_ref[1, 1])
    complexes = [
        (d[0] + gap, -d[2] - both),
        (e[0] - e[2], e[3] - e[1]),
        (d[0] - gap, d[2] - both),
    ]
    for n, (real_part, imag_part) in enumerate(complexes):
        wide[:, 2 * PART * (n + 1) : 2 * PART * (n + 2)] = times_table(
            jnp.concatenate([real_part, imag_part], axis=1), large_ref[0, n], large_ref[1, n]
        )
    low_lanes = lane_mask((rows, 4 * KEEP), 4 * KEEP, 2 * KEEP)
    for pair in range(fields // 2):
        for u in range(GRID // (4 * KEEP)):
            lanes = slice(4 * KEEP * u, 4 * KEEP * (u + 1))
            one = wide[2 * pair * rows : (2 * pair + 1) * rows, lanes]
            two = wide[(2 * pair + 1) * rows : (2 * pair + 2) * rows, lanes]
            out_ref[2 * u, pair] = jnp.where(low_lanes, one, pltpu.roll(two, 2 * KEEP, 1))
            out_ref[2 * u + 1, pair] = jnp.where(low_lanes, pltpu.roll(one, 2 * KEEP, 1), two)


def columns_kernel(special_ref, x_ref, across_ref, main_ref, extra_ref, mixed):
    devices, groups, rows, lanes = x_ref.shape
    special = special_ref[0] == 0
    step = 32

    @pl.loop(0, PART // step)
    def _(piece):
        for group in range(groups):
            parts = []
            extras = []
            for a in range(RADIX):
                start = a * PART + piece * step
                value = x_ref[start // rows, group, pl.ds(pl.multiple_of(start % rows, step), step), :]
                lane = lax.broadcasted_iota(jnp.int32, value.shape, 1) % (2 * KEEP)
                extras.append(
                    jnp.where(
                        jnp.logical_and(lane == 0, special), pltpu.roll(value, lanes - KEEP, 1), 0.0
                    )
                )
                parts.append(jnp.where(jnp.logical_and(lane == KEEP, special), 0.0, value))
            where = pl.ds(pl.multiple_of(piece * step, step), step)
            for k1, value in enumerate(eight(parts, minus_i)):
                mixed[k1, where, group * lanes : (group + 1) * lanes] = value
            for k1, value in enumerate(eight(extras, minus_i)):
                mixed[k1, where, (groups + group) * lanes : (groups + group + 1) * lanes] = value

    @pl.loop(0, RADIX)
    def _(k1):
        value = mixed[k1]
        both = jnp.concatenate([value, minus_i_wide(value)], axis=0)
        result = table_times(across_ref[0, k1], across_ref[1, k1], both)
        main_ref[k1] = result[:, : groups * lanes]
        extra_ref[k1] = result[:, groups * lanes :]


def minus_i_wide(values):
    width = 4 * KEEP
    return jnp.concatenate(
        [minus_i(values[:, start : start + width]) for start in range(0, values.shape[1], width)],
        axis=1,
    )


def pairs_kernel(numbers, main_ref, extra_ref, back_ref, out_ref, spread):
    lanes = 4 * KEEP
    tile = 32

    def forms(ref, k1, rows, field):
        group, side = field // 2, field % 2
        value = ref[k1, rows, group * lanes : (group + 1) * lanes]
        shape = value.shape
        turned = pltpu.roll(value, 2 * KEEP, 1)
        low = lane_mask(shape, lanes, 2 * KEEP)
        full = jnp.where(low, value, turned) if side == 0 else jnp.where(low, turned, value)
        forward, backward = pltpu.roll(full, lanes - KEEP, 1), pltpu.roll(full, KEEP, 1)
        real_lane = lane_mask(shape, 2 * KEEP, KEEP)
        real_part = jnp.where(real_lane, full, backward)
        imag_part = jnp.where(real_lane, forward, full)
        turned_part = jnp.where(real_lane, forward, -backward)
        return real_part, imag_part, full, turned_part

    used = [PAIRS[n] for q in numbers for n in (2 * q, 2 * q + 1) if n < len(PAIRS)]
    fields = sorted({f for pair in used for f in pair})

    @pl.loop(0, RADIX)
    def _(k1):
        @pl.loop(0, PART // tile)
        def _(piece):
            rows = pl.ds(pl.multiple_of(piece * tile, tile), tile)
            main = {f: forms(main_ref, k1, rows, f) for f in fields}
            extra = {f: forms(extra_ref, k1, rows, f) for f in fields}
            low = lane_mask((tile, lanes), lanes, 2 * KEEP)

            def cross(n):
                i, j = PAIRS[n]
                value = main[i][0] * main[j][2] + main[i][1] * main[j][3]
                return value + (extra[i][1] * extra[j][2] - extra[i][0] * extra[j][3])

            for place, q in enumerate(numbers):
                one = cross(2 * q)
                two = cross(2 * q + 1) if 2 * q + 1 < len(PAIRS) else jnp.zeros_like(one)
                value = jnp.where(low, one, two)
                spread[k1, rows, place * lanes : (place + 1) * lanes] = value

        value = spread[k1]
        both = jnp.concatenate([value, minus_i_wide(value)], axis=0)
        spread[k1] = table_times(back_ref[0, k1], back_ref[1, k1], both)

    block = out_ref.shape[2]

    @pl.loop(0, PART // tile)
    def _(piece):
        rows = pl.ds(pl.multiple_of(piece * tile, tile), tile)
        for place in range(len(numbers)):
            parts = [
                spread[k1, rows, place * lanes : (place + 1) * lanes] for k1 in range(RADIX)
            ]
            for a, value in enumerate(eight(parts, lambda v: -minus_i(v))):
                start = a * PART + piece * tile
                out_ref[
                    start // block, place, pl.ds(pl.multiple_of(start % block, tile), tile), :
                ] = value


def back_kernel(pair_count, x_ref, small_ref, large_ref, out_ref, wide):
    devices, groups, rows, lanes = x_ref.shape
    cols = out_ref.shape[3]
    per = cols // PART
    low_lanes = lane_mask((rows, lanes), lanes, 2 * KEEP)
    for place in range(pair_count):
        group, side = place // 2, place % 2
        for u in range(devices // 2):
            one, two = x_ref[2 * u, group], x_ref[2 * u + 1, group]
            if side == 0:
                value = jnp.where(low_lanes, one, pltpu.roll(two, 2 * KEEP, 1))
            else:
                value = jnp.where(low_lanes, pltpu.roll(one, 2 * KEEP, 1), two)
            wide[place * rows : (place + 1) * rows, lanes * u : lanes * (u + 1)] = value
    for place in range(pair_count):
        here = slice(place * rows, (place + 1) * rows)
        u0 = times_table(wide[here, 0:PART], small_ref[0, 0], small_ref[1, 0])
        u4 = times_table(wide[here, PART : 2 * PART], small_ref[0, 1], small_ref[1, 1])
        us = []
        for n in range(3):
            value = times_table(
                wide[here, 2 * PART * (n + 1) : 2 * PART * (n + 2)], large_ref[0, n], large_ref[1, n]
            )
            us.append((value[:, :PART], value[:, PART:]))
        (u1r, u1i), (u2r, u2i), (u3r, u3i) = us
        even, odd = u0 + u4, u0 - u4
        sums, gaps = even + u2r, even - u2r
        lefts, rights = odd - u2i, odd + u2i
        p0, p2 = u1r + u3r, u3i - u1i
        p1, p3 = ROOT * ((u1r - u1i) - (u3r + u3i)), ROOT * ((u3r - u3i) - (u1r + u1i))
        results = [
            sums + p0, lefts + p1, gaps + p2, rights + p3,
            sums - p0, lefts - p1, gaps - p2, rights - p3,
        ]
        for a, value in enumerate(results):
            out_ref[a // per, place, :, (a % per) * PART : (a % per + 1) * PART] = value


def call(body, shapes, scratch, in_specs=None, operands=()):
    count = len(operands)
    vmem = pl.BlockSpec(memory_space=pltpu.VMEM)
    return pl.pallas_call(
        body,
        out_shape=[jax.ShapeDtypeStruct(shape, jnp.float32) for shape in shapes],
        in_specs=in_specs or [vmem] * count,
        out_specs=[vmem] * len(shapes),
        scratch_shapes=[pltpu.VMEM(shape, jnp.float32) for shape in scratch],
        compiler_params=pltpu.CompilerParams(vmem_limit_bytes=VMEM_BYTES),
    )(*operands)


def pencil_local(labels, damage, opening, strain):
    small, large, small_back, large_back, across, across_back = [jnp.asarray(t) for t in tables()]
    phase_field = labels.astype(jnp.float32) - 1.0
    fields = jnp.concatenate([phase_field, damage, opening, strain[:, 0]], axis=0)
    field_count, row_count, cols = fields.shape
    sides = lax.axis_size("gy")
    devices = lax.axis_size("gx") * sides
    rows = row_count // sides
    sent = jnp.transpose(fields.reshape(field_count, sides, rows, cols), (1, 0, 2, 3))
    lines = lax.all_to_all(sent, "gy", split_axis=0, concat_axis=0)
    groups = field_count // 2
    lanes = 4 * KEEP
    (packed,) = call(
        rows_kernel,
        [(devices, groups, rows, lanes)],
        [(field_count * rows, GRID)],
        operands=(lines, small, large),
    )
    columns = lax.all_to_all(packed, ("gx", "gy"), split_axis=0, concat_axis=0)
    place = lax.axis_index("gx") * sides + lax.axis_index("gy")
    vmem = pl.BlockSpec(memory_space=pltpu.VMEM)
    spectrum_shape = (RADIX, PART, groups * lanes)
    main, extra = call(
        columns_kernel,
        [spectrum_shape, spectrum_shape],
        [(RADIX, PART, 2 * groups * lanes)],
        in_specs=[pl.BlockSpec(memory_space=pltpu.SMEM), vmem, vmem],
        operands=(place.astype(jnp.int32).reshape(1), columns, across),
    )
    results = []
    for begin, end in CHUNKS:
        numbers = tuple(range(begin, end))
        pair_count = min(2 * end, len(PAIRS)) - 2 * begin
        (crossed,) = call(
            functools.partial(pairs_kernel, numbers),
            [(devices, len(numbers), rows, lanes)],
            [(RADIX, PART, len(numbers) * lanes)],
            operands=(main, extra, across_back),
        )
        rows_of = lax.all_to_all(crossed, ("gx", "gy"), split_axis=0, concat_axis=0)
        (real_rows,) = call(
            functools.partial(back_kernel, pair_count),
            [(sides, pair_count, rows, cols)],
            [(pair_count * rows, GRID)],
            operands=(rows_of, small_back, large_back),
        )
        swapped = lax.all_to_all(real_rows, "gy", split_axis=0, concat_axis=0)
        results.append(
            jnp.transpose(swapped, (1, 0, 2, 3)).reshape(pair_count, 1, row_count, cols)
        )
    return jnp.concatenate(results, axis=0)


def fits_pencils(mesh):
    devices = mesh.shape["gx"] * mesh.shape["gy"]
    return devices * 2 * KEEP == GRID and GRID // mesh.shape["gy"] % PART == 0


def solution(mesh):
    in_specs = (
        P(None, "gx", "gy"),
        P(None, "gx", "gy"),
        P(None, "gx", "gy"),
        P(None, None, "gx", "gy"),
    )
    local = pencil_local if fits_pencils(mesh) else plain_local
    out_specs = P(None, None, "gx", "gy")
    return jax.shard_map(local, mesh=mesh, in_specs=in_specs, out_specs=out_specs, check_vma=False)
```

```python
import functools
import math

import jax
import jax.numpy as jnp
import ml_dtypes
import numpy as np
from jax import lax
from jax.experimental import pallas as pl
from jax.experimental.pallas import tpu as pltpu
from jax.sharding import PartitionSpec as P

GRID = 2048


HIGHEST = lax.Precision.HIGHEST


def phase_table(row_count, col_count, length, orient):
    row_index = lax.broadcasted_iota(jnp.int32, (row_count, col_count), 0)
    col_index = lax.broadcasted_iota(jnp.int32, (row_count, col_count), 1)
    angles = (row_index * col_index % length).astype(jnp.float32) * (2.0 * math.pi / length)
    return (jnp.cos(angles), orient * jnp.sin(angles))


def contract(stacked, factors, pattern):
    cosine, sine_part = factors

    def product(values, matrix):
        return jnp.einsum(
            pattern, values, matrix, precision=HIGHEST, preferred_element_type=jnp.float32
        )

    if stacked.shape[0] == 1:
        return jnp.stack([product(stacked[0], cosine), product(stacked[0], sine_part)])
    real_part, imag_part = (stacked[0], stacked[1])
    return jnp.stack(
        [
            product(real_part, cosine) - product(imag_part, sine_part),
            product(real_part, sine_part) + product(imag_part, cosine),
        ]
    )


def rotate(stacked, factors):
    cosine, sine_part = factors
    real_part, imag_part = (stacked[0], stacked[1])
    return jnp.stack(
        [real_part * cosine - imag_part * sine_part, real_part * sine_part + imag_part * cosine]
    )


def y_transform(stacked, orient):
    members, item_count, line_count, length = stacked.shape
    minor_size = 128
    major_size = length // minor_size
    blocks = stacked.reshape(members, item_count, line_count, major_size, minor_size)
    if orient < 0:
        blocks = contract(
            blocks, phase_table(major_size, major_size, major_size, orient), "bmuv,ku->bmkv"
        )
        blocks = rotate(blocks, phase_table(major_size, minor_size, length, orient))
        blocks = contract(
            blocks, phase_table(minor_size, minor_size, minor_size, orient), "bmkv,vn->bmkn"
        )
    else:
        blocks = contract(
            blocks, phase_table(minor_size, minor_size, minor_size, orient), "bmkn,nv->bmkv"
        )
        blocks = rotate(blocks, phase_table(major_size, minor_size, length, orient))
        blocks = contract(
            blocks, phase_table(major_size, major_size, major_size, orient), "bmkv,ku->bmuv"
        )
    return blocks.reshape(2, item_count, line_count, length)


def x_transform(stacked, orient):
    members, item_count, row_count, col_count = stacked.shape
    devices = lax.axis_size("gx")
    piece_size = row_count * col_count // devices
    device_index = lax.axis_index("gx")
    grid_size = row_count * devices
    frequency = lax.broadcasted_iota(jnp.int32, (devices, piece_size), 0)
    offset = lax.broadcasted_iota(jnp.int32, (devices, piece_size), 1)
    position = (device_index * piece_size + offset) // col_count
    angles = (position * frequency % grid_size).astype(jnp.float32) * (2.0 * math.pi / grid_size)
    twiddle = (jnp.cos(angles), orient * jnp.sin(angles))
    square = phase_table(devices, devices, devices, orient)
    if orient > 0:
        stacked = contract(
            stacked, phase_table(row_count, row_count, row_count, orient), "bkp,kr->brp"
        )

    def spread_work(received):
        if orient < 0:
            return rotate(contract(received, square, "bal,ka->bkl"), twiddle)
        return contract(rotate(received, twiddle), square, "bkl,ka->bal")

    spread = spread_work(
        lax.all_to_all(
            stacked.reshape(stacked.shape[0], item_count, devices, piece_size),
            "gx",
            split_axis=2,
            concat_axis=2,
            tiled=True,
        )
    )

    def collect_work(received):
        shaped = received.reshape(received.shape[0], received.shape[1], row_count, col_count)
        if orient < 0:
            return contract(
                shaped, phase_table(row_count, row_count, row_count, orient), "brp,kr->bkp"
            )
        return shaped

    return collect_work(lax.all_to_all(spread, "gx", split_axis=2, concat_axis=3, tiled=True))


def pencil_open(stacked, orient):
    return y_transform(
        lax.all_to_all(stacked, "gy", split_axis=2, concat_axis=3, tiled=True), orient
    )


def pencil_close(stacked):
    return lax.all_to_all(stacked, "gy", split_axis=3, concat_axis=2, tiled=True)


def pair_spectra(spectra, field_count, planes):
    members, item_count, line_count, length = spectra.shape
    shaped = spectra.reshape(2, field_count, planes, line_count, length)
    real_part, imag_part = (shaped[0], shaped[1])
    crosses = []
    for left_field in range(field_count):
        for right_field in range(left_field, field_count):
            crosses.append(
                (
                    real_part[left_field] * real_part[right_field]
                    + imag_part[left_field] * imag_part[right_field],
                    real_part[left_field] * imag_part[right_field]
                    - imag_part[left_field] * real_part[right_field],
                )
            )
    nothing = jnp.zeros_like(real_part[0])
    crosses.append((nothing, nothing))
    packed_real = []
    packed_imag = []
    for number in range(0, len(crosses), 2):
        even_pair = crosses[number]
        odd_pair = crosses[number + 1]
        packed_real.append(even_pair[0] - odd_pair[1])
        packed_imag.append(even_pair[1] + odd_pair[0])
    return jnp.stack([jnp.stack(packed_real), jnp.stack(packed_imag)]).reshape(
        2, -1, line_count, length
    )


def plain_local(labels, damage, opening, strain):
    phase_field = labels.astype(jnp.float32) - 1.0
    fields = jnp.concatenate([phase_field[None], damage[None], opening[None], strain], axis=0)
    field_count, planes, row_count, col_count = fields.shape
    stacked = fields.reshape(1, field_count * planes, row_count, col_count)
    spectra = pencil_open(x_transform(stacked, -1.0), -1.0)
    packed = pair_spectra(spectra, field_count, planes)
    result = x_transform(pencil_close(y_transform(packed, 1.0)), 1.0)
    pair_count = field_count * (field_count + 1) // 2
    shaped = result.reshape(2, -1, planes, row_count, col_count)
    alternated = jnp.stack([shaped[0], shaped[1]], axis=1).reshape(-1, planes, row_count, col_count)
    scale = 1.0 / (float(GRID) * float(GRID) * float(GRID))
    return alternated[:pair_count] * scale


RADIX = 8
PART = GRID // RADIX
FIELD_COUNT = 6
KEEP = 32
ROOT = math.sqrt(0.5)
PAIRS = [(i, j) for i in range(FIELD_COUNT) for j in range(i, FIELD_COUNT)]
CHUNKS = (
    (PAIRS[0:4],),
    (PAIRS[6:9], PAIRS[11:13], PAIRS[15:16]),
    (PAIRS[4:6], PAIRS[9:11], PAIRS[13:15]),
    (PAIRS[16:21],),
)
VMEM_BYTES = 56 * 1024 * 1024


def split_table(table):
    high = table.astype(np.float32).astype(ml_dtypes.bfloat16)
    low = (table - high.astype(np.float64)).astype(np.float32).astype(ml_dtypes.bfloat16)
    return np.stack([high, low])


def angle_table(first):
    b = np.arange(PART)[:, None]
    k2 = np.arange(PART)[None, :]
    return 2.0 * np.pi * ((b * (first + RADIX * k2)) % GRID) / GRID


def lane_order(values_real, values_imag):
    rows, count = values_real.shape
    both = np.stack([values_real.reshape(rows, -1, KEEP), values_imag.reshape(rows, -1, KEEP)], axis=2)
    return both.reshape(rows, 2 * count)


@functools.lru_cache(maxsize=None)
def tables():
    half = PART // 2
    small, large, small_back, large_back = [], [], [], []
    for first in (0, 4):
        angle = angle_table(first)[:, :half]
        cosine, sine = np.cos(angle), np.sin(angle)
        forward_imag = -sine
        back_real, back_imag = 2.0 * cosine, -2.0 * sine
        if first == 0:
            alternating = np.cos(np.pi * np.arange(PART))
            forward_imag[:, 0] = alternating
            back_real[:, 0] = 1.0
            back_imag[:, 0] = alternating
        small.append(lane_order(cosine, forward_imag))
        small_back.append(lane_order(back_real, back_imag).T)
    for first in (1, 2, 3):
        angle = angle_table(first)
        cosine, sine = np.cos(angle), np.sin(angle)
        large.append(np.concatenate([lane_order(cosine, -sine), lane_order(sine, cosine)], axis=0))
        large_back.append(
            2.0
            * np.concatenate([lane_order(cosine, -sine).T, lane_order(sine, cosine).T], axis=1)
        )
    scale = 1.0 / (float(GRID) * float(GRID) * float(GRID))
    across, across_back = [], []
    for first in range(RADIX):
        angle = angle_table(first)
        cosine, sine = np.cos(angle), np.sin(angle)
        across.append(np.concatenate([cosine.T, sine.T], axis=1))
        across_back.append(np.concatenate([cosine, -sine], axis=1))
    return tuple(
        split_table(np.stack(group))
        for group in (
            small,
            large,
            [scale * table for table in small_back],
            [scale * table for table in large_back],
            across,
            across_back,
        )
    )


def halves(values):
    high = values.astype(jnp.bfloat16)
    low = (values - high.astype(jnp.float32)).astype(jnp.bfloat16)
    return high, low


def dot(left, right):
    return jnp.dot(left, right, preferred_element_type=jnp.float32)


def times_table(values, table_high, table_low):
    high, low = halves(values)
    return dot(high, table_high) + (dot(low, table_high) + dot(high, table_low))


def table_times(table_high, table_low, values):
    high, low = halves(values)
    return dot(table_high, high) + (dot(table_high, low) + dot(table_low, high))


def lane_mask(shape, period, first):
    return lax.broadcasted_iota(jnp.int32, shape, 1) % period < first


def minus_i(values):
    real_lane = lane_mask(values.shape, 2 * KEEP, KEEP)
    width = values.shape[1]
    return jnp.where(
        real_lane, pltpu.roll(values, width - KEEP, 1), -pltpu.roll(values, KEEP, 1)
    )


def eight(parts, turn):
    e = [parts[a] + parts[a + 4] for a in range(4)]
    d = [parts[a] - parts[a + 4] for a in range(4)]
    even, odd = e[0] + e[2], e[1] + e[3]
    twist = turn(e[1] - e[3])
    flat = e[0] - e[2]
    cross = turn(d[2])
    near, far = d[0] + cross, d[0] - cross
    span = turn(d[1] + d[3])
    gap = d[1] - d[3]
    first, third = ROOT * (span + gap), ROOT * (span - gap)
    return [
        even + odd,
        near + first,
        flat + twist,
        far + third,
        even - odd,
        near - first,
        flat - twist,
        far - third,
    ]


def rows_kernel(x_ref, small_ref, large_ref, out_ref, wide):
    parts_count, fields, rows, cols = x_ref.shape
    per = cols // PART
    count = fields * rows

    def part(a):
        return x_ref[a // per, :, :, (a % per) * PART : (a % per + 1) * PART].reshape(count, PART)

    s = [part(a) for a in range(RADIX)]
    e = [s[a] + s[a + 4] for a in range(4)]
    d = [s[a] - s[a + 4] for a in range(4)]
    even, odd = e[0] + e[2], e[1] + e[3]
    gap, both = ROOT * (d[1] - d[3]), ROOT * (d[1] + d[3])
    wide[:, 0:PART] = times_table(even + odd, small_ref[0, 0], small_ref[1, 0])
    wide[:, PART : 2 * PART] = times_table(even - odd, small_ref[0, 1], small_ref[1, 1])
    complexes = [
        (d[0] + gap, -d[2] - both),
        (e[0] - e[2], e[3] - e[1]),
        (d[0] - gap, d[2] - both),
    ]
    for n, (real_part, imag_part) in enumerate(complexes):
        wide[:, 2 * PART * (n + 1) : 2 * PART * (n + 2)] = times_table(
            jnp.concatenate([real_part, imag_part], axis=1), large_ref[0, n], large_ref[1, n]
        )
    low_lanes = lane_mask((rows, 4 * KEEP), 4 * KEEP, 2 * KEEP)
    for pair in range(fields // 2):
        for u in range(GRID // (4 * KEEP)):
            lanes = slice(4 * KEEP * u, 4 * KEEP * (u + 1))
            one = wide[2 * pair * rows : (2 * pair + 1) * rows, lanes]
            two = wide[(2 * pair + 1) * rows : (2 * pair + 2) * rows, lanes]
            out_ref[2 * u, pair] = jnp.where(low_lanes, one, pltpu.roll(two, 2 * KEEP, 1))
            out_ref[2 * u + 1, pair] = jnp.where(low_lanes, pltpu.roll(one, 2 * KEEP, 1), two)


def columns_kernel(special_ref, x_ref, across_ref, main_ref, extra_ref, mixed):
    devices, groups, rows, lanes = x_ref.shape
    special = special_ref[0] == 0
    step = 32

    @pl.loop(0, PART // step)
    def _(piece):
        for group in range(groups):
            parts = []
            extras = []
            for a in range(RADIX):
                start = a * PART + piece * step
                value = x_ref[start // rows, group, pl.ds(pl.multiple_of(start % rows, step), step), :]
                lane = lax.broadcasted_iota(jnp.int32, value.shape, 1) % (2 * KEEP)
                extras.append(
                    jnp.where(
                        jnp.logical_and(lane == 0, special), pltpu.roll(value, lanes - KEEP, 1), 0.0
                    )
                )
                parts.append(jnp.where(jnp.logical_and(lane == KEEP, special), 0.0, value))
            where = pl.ds(pl.multiple_of(piece * step, step), step)
            for k1, value in enumerate(eight(parts, minus_i)):
                mixed[k1, where, group * lanes : (group + 1) * lanes] = value
            for k1, value in enumerate(eight(extras, minus_i)):
                mixed[k1, where, (groups + group) * lanes : (groups + group + 1) * lanes] = value

    @pl.loop(0, RADIX)
    def _(k1):
        value = mixed[k1]
        both = jnp.concatenate([value, minus_i_wide(value)], axis=0)
        result = table_times(across_ref[0, k1], across_ref[1, k1], both)
        main_ref[k1] = result[:, : groups * lanes]
        extra_ref[k1] = result[:, groups * lanes :]


def minus_i_wide(values):
    width = 4 * KEEP
    return jnp.concatenate(
        [minus_i(values[:, start : start + width]) for start in range(0, values.shape[1], width)],
        axis=1,
    )


def pairs_kernel(pairs, used, *refs):
    back_ref, out_ref, spread = refs[-3:]
    main_refs = {group: refs[2 * n] for n, group in enumerate(used)}
    extra_refs = {group: refs[2 * n + 1] for n, group in enumerate(used)}
    lanes = 4 * KEEP
    tile = 32
    groups = (len(pairs) + 1) // 2

    def forms(ref, k1, rows, field):
        value = ref[k1, rows, :]
        shape = value.shape
        turned = pltpu.roll(value, 2 * KEEP, 1)
        low = lane_mask(shape, lanes, 2 * KEEP)
        full = jnp.where(low, value, turned) if field % 2 == 0 else jnp.where(low, turned, value)
        forward, backward = pltpu.roll(full, lanes - KEEP, 1), pltpu.roll(full, KEEP, 1)
        real_lane = lane_mask(shape, 2 * KEEP, KEEP)
        real_part = jnp.where(real_lane, full, backward)
        imag_part = jnp.where(real_lane, forward, full)
        turned_part = jnp.where(real_lane, forward, -backward)
        return real_part, imag_part, full, turned_part

    fields = sorted({f for pair in pairs for f in pair})

    @pl.loop(0, RADIX)
    def _(k1):
        @pl.loop(0, PART // tile)
        def _(piece):
            rows = pl.ds(pl.multiple_of(piece * tile, tile), tile)
            main = {f: forms(main_refs[f // 2], k1, rows, f) for f in fields}
            extra = {f: forms(extra_refs[f // 2], k1, rows, f) for f in fields}
            low = lane_mask((tile, lanes), lanes, 2 * KEEP)

            def cross(n):
                i, j = pairs[n]
                value = main[i][0] * main[j][2] + main[i][1] * main[j][3]
                return value + (extra[i][1] * extra[j][2] - extra[i][0] * extra[j][3])

            for place in range(groups):
                one = cross(2 * place)
                two = cross(2 * place + 1) if 2 * place + 1 < len(pairs) else jnp.zeros_like(one)
                value = jnp.where(low, one, two)
                spread[k1, rows, place * lanes : (place + 1) * lanes] = value

        value = spread[k1]
        both = jnp.concatenate([value, minus_i_wide(value)], axis=0)
        spread[k1] = table_times(back_ref[0, k1], back_ref[1, k1], both)

    block = out_ref.shape[2]

    @pl.loop(0, PART // tile)
    def _(piece):
        rows = pl.ds(pl.multiple_of(piece * tile, tile), tile)
        for place in range(groups):
            parts = [
                spread[k1, rows, place * lanes : (place + 1) * lanes] for k1 in range(RADIX)
            ]
            for a, value in enumerate(eight(parts, lambda v: -minus_i(v))):
                start = a * PART + piece * tile
                out_ref[
                    start // block, place, pl.ds(pl.multiple_of(start % block, tile), tile), :
                ] = value


def back_kernel(pair_count, x_ref, small_ref, large_ref, out_ref, wide):
    devices, groups, rows, lanes = x_ref.shape
    cols = out_ref.shape[3]
    per = cols // PART
    low_lanes = lane_mask((rows, lanes), lanes, 2 * KEEP)
    for place in range(pair_count):
        group, side = place // 2, place % 2
        for u in range(devices // 2):
            one, two = x_ref[2 * u, group], x_ref[2 * u + 1, group]
            if side == 0:
                value = jnp.where(low_lanes, one, pltpu.roll(two, 2 * KEEP, 1))
            else:
                value = jnp.where(low_lanes, pltpu.roll(one, 2 * KEEP, 1), two)
            wide[place * rows : (place + 1) * rows, lanes * u : lanes * (u + 1)] = value
    for place in range(pair_count):
        here = slice(place * rows, (place + 1) * rows)
        u0 = times_table(wide[here, 0:PART], small_ref[0, 0], small_ref[1, 0])
        u4 = times_table(wide[here, PART : 2 * PART], small_ref[0, 1], small_ref[1, 1])
        us = []
        for n in range(3):
            value = times_table(
                wide[here, 2 * PART * (n + 1) : 2 * PART * (n + 2)], large_ref[0, n], large_ref[1, n]
            )
            us.append((value[:, :PART], value[:, PART:]))
        (u1r, u1i), (u2r, u2i), (u3r, u3i) = us
        even, odd = u0 + u4, u0 - u4
        sums, gaps = even + u2r, even - u2r
        lefts, rights = odd - u2i, odd + u2i
        p0, p2 = u1r + u3r, u3i - u1i
        p1, p3 = ROOT * ((u1r - u1i) - (u3r + u3i)), ROOT * ((u3r - u3i) - (u1r + u1i))
        results = [
            sums + p0, lefts + p1, gaps + p2, rights + p3,
            sums - p0, lefts - p1, gaps - p2, rights - p3,
        ]
        for a, value in enumerate(results):
            out_ref[a // per, place, :, (a % per) * PART : (a % per + 1) * PART] = value


def call(body, shapes, scratch, in_specs=None, operands=()):
    count = len(operands)
    vmem = pl.BlockSpec(memory_space=pltpu.VMEM)
    return pl.pallas_call(
        body,
        out_shape=[jax.ShapeDtypeStruct(shape, jnp.float32) for shape in shapes],
        in_specs=in_specs or [vmem] * count,
        out_specs=[vmem] * len(shapes),
        scratch_shapes=[pltpu.VMEM(shape, jnp.float32) for shape in scratch],
        compiler_params=pltpu.CompilerParams(vmem_limit_bytes=VMEM_BYTES),
    )(*operands)


def pencil_local(labels, damage, opening, strain):
    small, large, small_back, large_back, across, across_back = [jnp.asarray(t) for t in tables()]
    phase_field = labels.astype(jnp.float32) - 1.0
    row_count, cols = damage.shape[1:]
    sides = lax.axis_size("gy")
    devices = lax.axis_size("gx") * sides
    rows = row_count // sides
    lanes = 4 * KEEP
    side = lax.axis_index("gy")
    place = (lax.axis_index("gx") * sides + side).astype(jnp.int32).reshape(1)
    vmem = pl.BlockSpec(memory_space=pltpu.VMEM)
    swap = [(0, 1), (1, 0)]
    couples = [
        jnp.concatenate([phase_field, damage], axis=0),
        jnp.concatenate([opening, strain[0]], axis=0),
        strain[1:, 0],
    ]
    lines = []
    for couple in couples:
        kept = lax.dynamic_slice_in_dim(couple, side * rows, rows, axis=1)
        sent = lax.dynamic_slice_in_dim(couple, (1 - side) * rows, rows, axis=1)
        came = lax.ppermute(sent, "gy", swap)
        lines.append(
            jnp.stack([jnp.where(side == 0, kept, came), jnp.where(side == 0, came, kept)])
        )
    spectra = []
    spectrum_shape = (RADIX, PART, lanes)
    for line in lines:
        (packed,) = call(
            rows_kernel,
            [(devices, 1, rows, lanes)],
            [(2 * rows, GRID)],
            operands=(line, small, large),
        )
        columns = lax.all_to_all(packed, ("gx", "gy"), split_axis=0, concat_axis=0)
        spectra.append(
            call(
                columns_kernel,
                [spectrum_shape, spectrum_shape],
                [(RADIX, PART, 2 * lanes)],
                in_specs=[pl.BlockSpec(memory_space=pltpu.SMEM), vmem, vmem],
                operands=(place, columns, across),
            )
        )
    crosses = []
    for chunk in CHUNKS:
        pairs = [pair for run in chunk for pair in run]
        groups = (len(pairs) + 1) // 2
        used = sorted({field // 2 for pair in pairs for field in pair})
        (crossed,) = call(
            functools.partial(pairs_kernel, pairs, used),
            [(devices, groups, rows, lanes)],
            [(RADIX, PART, groups * lanes)],
            operands=tuple(part for n in used for part in spectra[n]) + (across_back,),
        )
        crosses.append(crossed)
    result = jnp.zeros((len(PAIRS), row_count, cols), jnp.float32)
    for n, chunk in enumerate(CHUNKS):
        pair_count = sum(len(run) for run in chunk)
        rows_of = lax.all_to_all(crosses[n], ("gx", "gy"), split_axis=0, concat_axis=0)
        (real_rows,) = call(
            functools.partial(back_kernel, pair_count),
            [(sides, pair_count, rows, cols)],
            [(pair_count * rows, GRID)],
            operands=(rows_of, small_back, large_back),
        )
        sent = lax.dynamic_index_in_dim(real_rows, 1 - side, 0, keepdims=False)
        kept = lax.dynamic_index_in_dim(real_rows, side, 0, keepdims=False)
        came = lax.ppermute(sent, "gy", swap)
        if n + 2 < len(CHUNKS):
            came, crosses[n + 2] = lax.optimization_barrier((came, crosses[n + 2]))
        for half in range(2):
            values = jnp.where(side == half, kept, came)
            begin = 0
            for run in chunk:
                first = PAIRS.index(run[0])
                result = lax.dynamic_update_slice(
                    result, values[begin : begin + len(run)], (first, half * rows, 0)
                )
                begin += len(run)
    return result.reshape(len(PAIRS), 1, row_count, cols)


def fits_pencils(mesh):
    devices = mesh.shape["gx"] * mesh.shape["gy"]
    return devices * 2 * KEEP == GRID and mesh.shape["gy"] == 2


def solution(mesh):
    in_specs = (
        P(None, "gx", "gy"),
        P(None, "gx", "gy"),
        P(None, "gx", "gy"),
        P(None, None, "gx", "gy"),
    )
    local = pencil_local if fits_pencils(mesh) else plain_local
    out_specs = P(None, None, "gx", "gy")
    return jax.shard_map(local, mesh=mesh, in_specs=in_specs, out_specs=out_specs, check_vma=False)
```

```python
import functools
import math

import jax
import jax.numpy as jnp
import ml_dtypes
import numpy as np
from jax import lax
from jax.experimental import pallas as pl
from jax.experimental.pallas import tpu as pltpu
from jax.sharding import PartitionSpec as P

GRID = 2048


HIGHEST = lax.Precision.HIGHEST


def phase_table(row_count, col_count, length, orient):
    row_index = lax.broadcasted_iota(jnp.int32, (row_count, col_count), 0)
    col_index = lax.broadcasted_iota(jnp.int32, (row_count, col_count), 1)
    angles = (row_index * col_index % length).astype(jnp.float32) * (2.0 * math.pi / length)
    return (jnp.cos(angles), orient * jnp.sin(angles))


def contract(stacked, factors, pattern):
    cosine, sine_part = factors

    def product(values, matrix):
        return jnp.einsum(
            pattern, values, matrix, precision=HIGHEST, preferred_element_type=jnp.float32
        )

    if stacked.shape[0] == 1:
        return jnp.stack([product(stacked[0], cosine), product(stacked[0], sine_part)])
    real_part, imag_part = (stacked[0], stacked[1])
    return jnp.stack(
        [
            product(real_part, cosine) - product(imag_part, sine_part),
            product(real_part, sine_part) + product(imag_part, cosine),
        ]
    )


def rotate(stacked, factors):
    cosine, sine_part = factors
    real_part, imag_part = (stacked[0], stacked[1])
    return jnp.stack(
        [real_part * cosine - imag_part * sine_part, real_part * sine_part + imag_part * cosine]
    )


def y_transform(stacked, orient):
    members, item_count, line_count, length = stacked.shape
    minor_size = 128
    major_size = length // minor_size
    blocks = stacked.reshape(members, item_count, line_count, major_size, minor_size)
    if orient < 0:
        blocks = contract(
            blocks, phase_table(major_size, major_size, major_size, orient), "bmuv,ku->bmkv"
        )
        blocks = rotate(blocks, phase_table(major_size, minor_size, length, orient))
        blocks = contract(
            blocks, phase_table(minor_size, minor_size, minor_size, orient), "bmkv,vn->bmkn"
        )
    else:
        blocks = contract(
            blocks, phase_table(minor_size, minor_size, minor_size, orient), "bmkn,nv->bmkv"
        )
        blocks = rotate(blocks, phase_table(major_size, minor_size, length, orient))
        blocks = contract(
            blocks, phase_table(major_size, major_size, major_size, orient), "bmkv,ku->bmuv"
        )
    return blocks.reshape(2, item_count, line_count, length)


def x_transform(stacked, orient):
    members, item_count, row_count, col_count = stacked.shape
    devices = lax.axis_size("gx")
    piece_size = row_count * col_count // devices
    device_index = lax.axis_index("gx")
    grid_size = row_count * devices
    frequency = lax.broadcasted_iota(jnp.int32, (devices, piece_size), 0)
    offset = lax.broadcasted_iota(jnp.int32, (devices, piece_size), 1)
    position = (device_index * piece_size + offset) // col_count
    angles = (position * frequency % grid_size).astype(jnp.float32) * (2.0 * math.pi / grid_size)
    twiddle = (jnp.cos(angles), orient * jnp.sin(angles))
    square = phase_table(devices, devices, devices, orient)
    if orient > 0:
        stacked = contract(
            stacked, phase_table(row_count, row_count, row_count, orient), "bkp,kr->brp"
        )

    def spread_work(received):
        if orient < 0:
            return rotate(contract(received, square, "bal,ka->bkl"), twiddle)
        return contract(rotate(received, twiddle), square, "bkl,ka->bal")

    spread = spread_work(
        lax.all_to_all(
            stacked.reshape(stacked.shape[0], item_count, devices, piece_size),
            "gx",
            split_axis=2,
            concat_axis=2,
            tiled=True,
        )
    )

    def collect_work(received):
        shaped = received.reshape(received.shape[0], received.shape[1], row_count, col_count)
        if orient < 0:
            return contract(
                shaped, phase_table(row_count, row_count, row_count, orient), "brp,kr->bkp"
            )
        return shaped

    return collect_work(lax.all_to_all(spread, "gx", split_axis=2, concat_axis=3, tiled=True))


def pencil_open(stacked, orient):
    return y_transform(
        lax.all_to_all(stacked, "gy", split_axis=2, concat_axis=3, tiled=True), orient
    )


def pencil_close(stacked):
    return lax.all_to_all(stacked, "gy", split_axis=3, concat_axis=2, tiled=True)


def pair_spectra(spectra, field_count, planes):
    members, item_count, line_count, length = spectra.shape
    shaped = spectra.reshape(2, field_count, planes, line_count, length)
    real_part, imag_part = (shaped[0], shaped[1])
    crosses = []
    for left_field in range(field_count):
        for right_field in range(left_field, field_count):
            crosses.append(
                (
                    real_part[left_field] * real_part[right_field]
                    + imag_part[left_field] * imag_part[right_field],
                    real_part[left_field] * imag_part[right_field]
                    - imag_part[left_field] * real_part[right_field],
                )
            )
    nothing = jnp.zeros_like(real_part[0])
    crosses.append((nothing, nothing))
    packed_real = []
    packed_imag = []
    for number in range(0, len(crosses), 2):
        even_pair = crosses[number]
        odd_pair = crosses[number + 1]
        packed_real.append(even_pair[0] - odd_pair[1])
        packed_imag.append(even_pair[1] + odd_pair[0])
    return jnp.stack([jnp.stack(packed_real), jnp.stack(packed_imag)]).reshape(
        2, -1, line_count, length
    )


def plain_local(labels, damage, opening, strain):
    phase_field = labels.astype(jnp.float32) - 1.0
    fields = jnp.concatenate([phase_field[None], damage[None], opening[None], strain], axis=0)
    field_count, planes, row_count, col_count = fields.shape
    stacked = fields.reshape(1, field_count * planes, row_count, col_count)
    spectra = pencil_open(x_transform(stacked, -1.0), -1.0)
    packed = pair_spectra(spectra, field_count, planes)
    result = x_transform(pencil_close(y_transform(packed, 1.0)), 1.0)
    pair_count = field_count * (field_count + 1) // 2
    shaped = result.reshape(2, -1, planes, row_count, col_count)
    alternated = jnp.stack([shaped[0], shaped[1]], axis=1).reshape(-1, planes, row_count, col_count)
    scale = 1.0 / (float(GRID) * float(GRID) * float(GRID))
    return alternated[:pair_count] * scale


RADIX = 8
PART = GRID // RADIX
FIELD_COUNT = 6
KEEP = 32
ROOT = math.sqrt(0.5)
PAIRS = [(i, j) for i in range(FIELD_COUNT) for j in range(i, FIELD_COUNT)]
CHUNKS = (
    (PAIRS[0:4],),
    (PAIRS[6:9], PAIRS[11:13], PAIRS[15:16], PAIRS[4:6]),
    (PAIRS[9:11], PAIRS[13:15], PAIRS[16:18]),
    (PAIRS[18:21],),
)
VMEM_BYTES = 56 * 1024 * 1024


def split_table(table):
    high = table.astype(np.float32).astype(ml_dtypes.bfloat16)
    low = (table - high.astype(np.float64)).astype(np.float32).astype(ml_dtypes.bfloat16)
    return np.stack([high, low])


def angle_table(first):
    b = np.arange(PART)[:, None]
    k2 = np.arange(PART)[None, :]
    return 2.0 * np.pi * ((b * (first + RADIX * k2)) % GRID) / GRID


def lane_order(values_real, values_imag):
    rows, count = values_real.shape
    both = np.stack([values_real.reshape(rows, -1, KEEP), values_imag.reshape(rows, -1, KEEP)], axis=2)
    return both.reshape(rows, 2 * count)


@functools.lru_cache(maxsize=None)
def tables():
    half = PART // 2
    small, large, small_back, large_back = [], [], [], []
    for first in (0, 4):
        angle = angle_table(first)[:, :half]
        cosine, sine = np.cos(angle), np.sin(angle)
        forward_imag = -sine
        back_real, back_imag = 2.0 * cosine, -2.0 * sine
        if first == 0:
            alternating = np.cos(np.pi * np.arange(PART))
            forward_imag[:, 0] = alternating
            back_real[:, 0] = 1.0
            back_imag[:, 0] = alternating
        small.append(lane_order(cosine, forward_imag))
        small_back.append(lane_order(back_real, back_imag).T)
    for first in (1, 2, 3):
        angle = angle_table(first)
        cosine, sine = np.cos(angle), np.sin(angle)
        large.append(np.concatenate([lane_order(cosine, -sine), lane_order(sine, cosine)], axis=0))
        large_back.append(
            2.0
            * np.concatenate([lane_order(cosine, -sine).T, lane_order(sine, cosine).T], axis=1)
        )
    scale = 1.0 / (float(GRID) * float(GRID) * float(GRID))
    across, across_back = [], []
    for first in range(RADIX):
        angle = angle_table(first)
        cosine, sine = np.cos(angle), np.sin(angle)
        across.append(np.concatenate([cosine.T, sine.T], axis=1))
        across_back.append(np.concatenate([cosine, -sine], axis=1))
    return tuple(
        split_table(np.stack(group))
        for group in (
            small,
            large,
            [scale * table for table in small_back],
            [scale * table for table in large_back],
            across,
            across_back,
        )
    )


def halves(values):
    high = values.astype(jnp.bfloat16)
    low = (values - high.astype(jnp.float32)).astype(jnp.bfloat16)
    return high, low


def dot(left, right):
    return jnp.dot(left, right, preferred_element_type=jnp.float32)


def times_table(values, table_high, table_low):
    high, low = halves(values)
    return dot(high, table_high) + (dot(low, table_high) + dot(high, table_low))


def table_times(table_high, table_low, values):
    high, low = halves(values)
    return dot(table_high, high) + (dot(table_high, low) + dot(table_low, high))


def lane_mask(shape, period, first):
    return lax.broadcasted_iota(jnp.int32, shape, 1) % period < first


def minus_i(values):
    real_lane = lane_mask(values.shape, 2 * KEEP, KEEP)
    width = values.shape[1]
    return jnp.where(
        real_lane, pltpu.roll(values, width - KEEP, 1), -pltpu.roll(values, KEEP, 1)
    )


def eight(parts, turn):
    e = [parts[a] + parts[a + 4] for a in range(4)]
    d = [parts[a] - parts[a + 4] for a in range(4)]
    even, odd = e[0] + e[2], e[1] + e[3]
    twist = turn(e[1] - e[3])
    flat = e[0] - e[2]
    cross = turn(d[2])
    near, far = d[0] + cross, d[0] - cross
    span = turn(d[1] + d[3])
    gap = d[1] - d[3]
    first, third = ROOT * (span + gap), ROOT * (span - gap)
    return [
        even + odd,
        near + first,
        flat + twist,
        far + third,
        even - odd,
        near - first,
        flat - twist,
        far - third,
    ]


def rows_kernel(x_ref, small_ref, large_ref, out_ref, wide):
    parts_count, fields, rows, cols = x_ref.shape
    per = cols // PART
    count = fields * rows

    def part(a):
        return x_ref[a // per, :, :, (a % per) * PART : (a % per + 1) * PART].reshape(count, PART)

    s = [part(a) for a in range(RADIX)]
    e = [s[a] + s[a + 4] for a in range(4)]
    d = [s[a] - s[a + 4] for a in range(4)]
    even, odd = e[0] + e[2], e[1] + e[3]
    gap, both = ROOT * (d[1] - d[3]), ROOT * (d[1] + d[3])
    wide[:, 0:PART] = times_table(even + odd, small_ref[0, 0], small_ref[1, 0])
    wide[:, PART : 2 * PART] = times_table(even - odd, small_ref[0, 1], small_ref[1, 1])
    complexes = [
        (d[0] + gap, -d[2] - both),
        (e[0] - e[2], e[3] - e[1]),
        (d[0] - gap, d[2] - both),
    ]
    for n, (real_part, imag_part) in enumerate(complexes):
        wide[:, 2 * PART * (n + 1) : 2 * PART * (n + 2)] = times_table(
            jnp.concatenate([real_part, imag_part], axis=1), large_ref[0, n], large_ref[1, n]
        )
    low_lanes = lane_mask((rows, 4 * KEEP), 4 * KEEP, 2 * KEEP)
    for pair in range(fields // 2):
        for u in range(GRID // (4 * KEEP)):
            lanes = slice(4 * KEEP * u, 4 * KEEP * (u + 1))
            one = wide[2 * pair * rows : (2 * pair + 1) * rows, lanes]
            two = wide[(2 * pair + 1) * rows : (2 * pair + 2) * rows, lanes]
            out_ref[2 * u, pair] = jnp.where(low_lanes, one, pltpu.roll(two, 2 * KEEP, 1))
            out_ref[2 * u + 1, pair] = jnp.where(low_lanes, pltpu.roll(one, 2 * KEEP, 1), two)


def columns_kernel(special_ref, x_ref, across_ref, main_ref, extra_ref, mixed):
    devices, groups, rows, lanes = x_ref.shape
    special = special_ref[0] == 0
    step = 32

    @pl.loop(0, PART // step)
    def _(piece):
        for group in range(groups):
            parts = []
            extras = []
            for a in range(RADIX):
                start = a * PART + piece * step
                value = x_ref[start // rows, group, pl.ds(pl.multiple_of(start % rows, step), step), :]
                lane = lax.broadcasted_iota(jnp.int32, value.shape, 1) % (2 * KEEP)
                extras.append(
                    jnp.where(
                        jnp.logical_and(lane == 0, special), pltpu.roll(value, lanes - KEEP, 1), 0.0
                    )
                )
                parts.append(jnp.where(jnp.logical_and(lane == KEEP, special), 0.0, value))
            where = pl.ds(pl.multiple_of(piece * step, step), step)
            for k1, value in enumerate(eight(parts, minus_i)):
                mixed[k1, where, group * lanes : (group + 1) * lanes] = value
            for k1, value in enumerate(eight(extras, minus_i)):
                mixed[k1, where, (groups + group) * lanes : (groups + group + 1) * lanes] = value

    @pl.loop(0, RADIX)
    def _(k1):
        value = mixed[k1]
        both = jnp.concatenate([value, minus_i_wide(value)], axis=0)
        result = table_times(across_ref[0, k1], across_ref[1, k1], both)
        main_ref[k1] = result[:, : groups * lanes]
        extra_ref[k1] = result[:, groups * lanes :]


def minus_i_wide(values):
    width = 4 * KEEP
    return jnp.concatenate(
        [minus_i(values[:, start : start + width]) for start in range(0, values.shape[1], width)],
        axis=1,
    )


def pairs_kernel(pairs, used, *refs):
    back_ref, out_ref, spread = refs[-3:]
    main_refs = {group: refs[2 * n] for n, group in enumerate(used)}
    extra_refs = {group: refs[2 * n + 1] for n, group in enumerate(used)}
    lanes = 4 * KEEP
    tile = 32
    groups = (len(pairs) + 1) // 2

    def forms(ref, k1, rows, field):
        value = ref[k1, rows, :]
        shape = value.shape
        turned = pltpu.roll(value, 2 * KEEP, 1)
        low = lane_mask(shape, lanes, 2 * KEEP)
        full = jnp.where(low, value, turned) if field % 2 == 0 else jnp.where(low, turned, value)
        forward, backward = pltpu.roll(full, lanes - KEEP, 1), pltpu.roll(full, KEEP, 1)
        real_lane = lane_mask(shape, 2 * KEEP, KEEP)
        real_part = jnp.where(real_lane, full, backward)
        imag_part = jnp.where(real_lane, forward, full)
        turned_part = jnp.where(real_lane, forward, -backward)
        return real_part, imag_part, full, turned_part

    fields = sorted({f for pair in pairs for f in pair})

    @pl.loop(0, RADIX)
    def _(k1):
        @pl.loop(0, PART // tile)
        def _(piece):
            rows = pl.ds(pl.multiple_of(piece * tile, tile), tile)
            main = {f: forms(main_refs[f // 2], k1, rows, f) for f in fields}
            extra = {f: forms(extra_refs[f // 2], k1, rows, f) for f in fields}
            low = lane_mask((tile, lanes), lanes, 2 * KEEP)

            def cross(n):
                i, j = pairs[n]
                value = main[i][0] * main[j][2] + main[i][1] * main[j][3]
                return value + (extra[i][1] * extra[j][2] - extra[i][0] * extra[j][3])

            for place in range(groups):
                one = cross(2 * place)
                two = cross(2 * place + 1) if 2 * place + 1 < len(pairs) else jnp.zeros_like(one)
                value = jnp.where(low, one, two)
                spread[k1, rows, place * lanes : (place + 1) * lanes] = value

        value = spread[k1]
        both = jnp.concatenate([value, minus_i_wide(value)], axis=0)
        spread[k1] = table_times(back_ref[0, k1], back_ref[1, k1], both)

    block = out_ref.shape[2]

    @pl.loop(0, PART // tile)
    def _(piece):
        rows = pl.ds(pl.multiple_of(piece * tile, tile), tile)
        for place in range(groups):
            parts = [
                spread[k1, rows, place * lanes : (place + 1) * lanes] for k1 in range(RADIX)
            ]
            for a, value in enumerate(eight(parts, lambda v: -minus_i(v))):
                start = a * PART + piece * tile
                out_ref[
                    start // block, place, pl.ds(pl.multiple_of(start % block, tile), tile), :
                ] = value


def back_kernel(pair_count, x_ref, small_ref, large_ref, out_ref, wide):
    devices, groups, rows, lanes = x_ref.shape
    cols = out_ref.shape[3]
    per = cols // PART
    low_lanes = lane_mask((rows, lanes), lanes, 2 * KEEP)
    for place in range(pair_count):
        group, side = place // 2, place % 2
        for u in range(devices // 2):
            one, two = x_ref[2 * u, group], x_ref[2 * u + 1, group]
            if side == 0:
                value = jnp.where(low_lanes, one, pltpu.roll(two, 2 * KEEP, 1))
            else:
                value = jnp.where(low_lanes, pltpu.roll(one, 2 * KEEP, 1), two)
            wide[place * rows : (place + 1) * rows, lanes * u : lanes * (u + 1)] = value
    for place in range(pair_count):
        here = slice(place * rows, (place + 1) * rows)
        u0 = times_table(wide[here, 0:PART], small_ref[0, 0], small_ref[1, 0])
        u4 = times_table(wide[here, PART : 2 * PART], small_ref[0, 1], small_ref[1, 1])
        us = []
        for n in range(3):
            value = times_table(
                wide[here, 2 * PART * (n + 1) : 2 * PART * (n + 2)], large_ref[0, n], large_ref[1, n]
            )
            us.append((value[:, :PART], value[:, PART:]))
        (u1r, u1i), (u2r, u2i), (u3r, u3i) = us
        even, odd = u0 + u4, u0 - u4
        sums, gaps = even + u2r, even - u2r
        lefts, rights = odd - u2i, odd + u2i
        p0, p2 = u1r + u3r, u3i - u1i
        p1, p3 = ROOT * ((u1r - u1i) - (u3r + u3i)), ROOT * ((u3r - u3i) - (u1r + u1i))
        results = [
            sums + p0, lefts + p1, gaps + p2, rights + p3,
            sums - p0, lefts - p1, gaps - p2, rights - p3,
        ]
        for a, value in enumerate(results):
            out_ref[a // per, place, :, (a % per) * PART : (a % per + 1) * PART] = value


def call(body, shapes, scratch, in_specs=None, operands=()):
    count = len(operands)
    vmem = pl.BlockSpec(memory_space=pltpu.VMEM)
    return pl.pallas_call(
        body,
        out_shape=[jax.ShapeDtypeStruct(shape, jnp.float32) for shape in shapes],
        in_specs=in_specs or [vmem] * count,
        out_specs=[vmem] * len(shapes),
        scratch_shapes=[pltpu.VMEM(shape, jnp.float32) for shape in scratch],
        compiler_params=pltpu.CompilerParams(vmem_limit_bytes=VMEM_BYTES),
    )(*operands)


def pencil_local(labels, damage, opening, strain):
    small, large, small_back, large_back, across, across_back = [jnp.asarray(t) for t in tables()]
    phase_field = labels.astype(jnp.float32) - 1.0
    row_count, cols = damage.shape[1:]
    sides = lax.axis_size("gy")
    devices = lax.axis_size("gx") * sides
    rows = row_count // sides
    lanes = 4 * KEEP
    side = lax.axis_index("gy")
    place = (lax.axis_index("gx") * sides + side).astype(jnp.int32).reshape(1)
    vmem = pl.BlockSpec(memory_space=pltpu.VMEM)
    swap = [(0, 1), (1, 0)]
    couples = [
        jnp.concatenate([phase_field, damage], axis=0),
        jnp.concatenate([opening, strain[0]], axis=0),
        strain[1:, 0],
    ]
    lines = []
    for couple in couples:
        kept = lax.dynamic_slice_in_dim(couple, side * rows, rows, axis=1)
        sent = lax.dynamic_slice_in_dim(couple, (1 - side) * rows, rows, axis=1)
        came = lax.ppermute(sent, "gy", swap)
        lines.append(
            jnp.stack([jnp.where(side == 0, kept, came), jnp.where(side == 0, came, kept)])
        )
    spectra = []
    spectrum_shape = (RADIX, PART, lanes)
    for line in lines:
        (packed,) = call(
            rows_kernel,
            [(devices, 1, rows, lanes)],
            [(2 * rows, GRID)],
            operands=(line, small, large),
        )
        if len(spectra) == 2:
            spectra[0], packed = lax.optimization_barrier((spectra[0], packed))
        columns = lax.all_to_all(packed, ("gx", "gy"), split_axis=0, concat_axis=0)
        spectra.append(
            call(
                columns_kernel,
                [spectrum_shape, spectrum_shape],
                [(RADIX, PART, 2 * lanes)],
                in_specs=[pl.BlockSpec(memory_space=pltpu.SMEM), vmem, vmem],
                operands=(place, columns, across),
            )
        )
    crosses = []
    for chunk in CHUNKS:
        pairs = [pair for run in chunk for pair in run]
        groups = (len(pairs) + 1) // 2
        used = sorted({field // 2 for pair in pairs for field in pair})
        (crossed,) = call(
            functools.partial(pairs_kernel, pairs, used),
            [(devices, groups, rows, lanes)],
            [(RADIX, PART, groups * lanes)],
            operands=tuple(part for n in used for part in spectra[n]) + (across_back,),
        )
        crosses.append(crossed)
    result = jnp.zeros((len(PAIRS), row_count, cols), jnp.float32)
    for n, chunk in enumerate(CHUNKS):
        pair_count = sum(len(run) for run in chunk)
        rows_of = lax.all_to_all(crosses[n], ("gx", "gy"), split_axis=0, concat_axis=0)
        (real_rows,) = call(
            functools.partial(back_kernel, pair_count),
            [(sides, pair_count, rows, cols)],
            [(pair_count * rows, GRID)],
            operands=(rows_of, small_back, large_back),
        )
        sent = lax.dynamic_index_in_dim(real_rows, 1 - side, 0, keepdims=False)
        kept = lax.dynamic_index_in_dim(real_rows, side, 0, keepdims=False)
        came = lax.ppermute(sent, "gy", swap)
        if n + 2 < len(CHUNKS):
            came, crosses[n + 2] = lax.optimization_barrier((came, crosses[n + 2]))
        for half in range(2):
            values = jnp.where(side == half, kept, came)
            begin = 0
            for run in chunk:
                first = PAIRS.index(run[0])
                result = lax.dynamic_update_slice(
                    result, values[begin : begin + len(run)], (first, half * rows, 0)
                )
                begin += len(run)
    return result.reshape(len(PAIRS), 1, row_count, cols)


def fits_pencils(mesh):
    devices = mesh.shape["gx"] * mesh.shape["gy"]
    return devices * 2 * KEEP == GRID and mesh.shape["gy"] == 2


def solution(mesh):
    in_specs = (
        P(None, "gx", "gy"),
        P(None, "gx", "gy"),
        P(None, "gx", "gy"),
        P(None, None, "gx", "gy"),
    )
    local = pencil_local if fits_pencils(mesh) else plain_local
    out_specs = P(None, None, "gx", "gy")
    return jax.shard_map(local, mesh=mesh, in_specs=in_specs, out_specs=out_specs, check_vma=False)
```
